256 devices in a mesh: tok: 4 (over y), row: 8 (over z_hi, core), col: 8 (over z_lo, x).
Axes of the slice: x: 4, y: 4, z: 8 (z_hi: 4, z_lo: 2; z = z_hi * 2 + z_lo), core: 2. Of those that a mesh axis runs over, the one named last changes fastest.
Arguments:
- tokens: bfloat16 [1024, 8192], P('tok', ('row', 'col')), may hold values from -6 to 6
- gate_weight: bfloat16 [8192, 14336], P('row', ('col', 'tok')), may hold values from -0.0625 to 0.0625
- up_weight: bfloat16 [8192, 14336], P('row', ('col', 'tok')), may hold values from -0.0625 to 0.0625
- down_weight: bfloat16 [14336, 8192], P(('col', 'tok'), 'row'), may hold values from -0.046875 to 0.046875
- cotangent: bfloat16 [1024, 8192], P('tok', ('row', 'col')), may hold values from -6 to 6
Outputs:
- block_out: bfloat16 [1024, 8192], P('tok', ('row', 'col'))
- input_grad: bfloat16 [1024, 8192], P('tok', ('row', 'col'))
- gate_grad: bfloat16 [8192, 14336], P('row', ('col', 'tok'))
- up_grad: bfloat16 [8192, 14336], P('row', ('col', 'tok'))
- down_grad: bfloat16 [14336, 8192], P(('col', 'tok'), 'row')
The draws below stay inside these ranges and needn't reach their ends.
All inputs are finite; a program needn't handle non-finite values.
Results may differ from the reference program's by a relative error of at most 0.0049.
Values may be sent and summed in bfloat16 or wider, within the bound.
A program may use at most 128 MiB of HBM per device.

```python
import jax
import jax.numpy as jnp

D = 8192
FF = 14336
TOKENS = 1024


def steps_of(own_key, dims, pieces, least, high):
    level = 1.0
    for dim, parts in pieces:
        steps = jax.random.uniform(jax.random.fold_in(jax.random.fold_in(own_key, 6), dim), (parts,), jnp.float32, least / len(pieces), high / len(pieces))
        level = level * jnp.repeat(jnp.exp(steps), dims[dim] // parts).reshape((-1,) + (1,) * (len(dims) - 1 - dim))
    return level


def normal_values(key, dims, spread, reach, shards=(), kind=jnp.bfloat16):
    entries = spread * jax.random.normal(key, dims, jnp.float32)
    if shards:
        entries = entries * steps_of(key, dims, shards, -0.22, 0.18)
    return jnp.clip(entries, -reach, reach).astype(kind)


def setup_inputs(seed: int = 0) -> dict:
    splits = jax.random.split(jax.random.key(seed), 6)
    return {
        "tokens": normal_values(splits[0], (TOKENS, D), 1.0, 6.0, ((0, 4), (1, 64))),
        "gate_weight": normal_values(splits[1], (D, FF), D ** -0.5, 0.0625, ((0, 8), (1, 32))),
        "up_weight": normal_values(splits[2], (D, FF), D ** -0.5, 0.0625, ((0, 8), (1, 32))),
        "down_weight": normal_values(splits[3], (FF, D), FF ** -0.5, 0.046875, ((0, 32), (1, 8))),
        "cotangent": normal_values(splits[4], (TOKENS, D), 1.0, 6.0, ((0, 4), (1, 64))),
    }


def reference(tokens, gate_weight, up_weight, down_weight, cotangent):
    gate_sum = jnp.dot(tokens, gate_weight, preferred_element_type=jnp.float32)
    up_sum = jnp.dot(tokens, up_weight, preferred_element_type=jnp.float32)
    squash = jax.nn.sigmoid(gate_sum)
    swish = gate_sum * squash
    hidden = (swish * up_sum).astype(jnp.bfloat16)
    block_out = jnp.dot(hidden, down_weight, preferred_element_type=jnp.float32).astype(jnp.bfloat16)
    slope = jnp.dot(cotangent, down_weight.T, preferred_element_type=jnp.float32)
    gate_slope = (slope * up_sum * squash * (1.0 + gate_sum * (1.0 - squash))).astype(jnp.bfloat16)
    up_slope = (slope * swish).astype(jnp.bfloat16)
    input_grad = (jnp.dot(gate_slope, gate_weight.T, preferred_element_type=jnp.float32)
                  + jnp.dot(up_slope, up_weight.T, preferred_element_type=jnp.float32)).astype(jnp.bfloat16)
    gate_total = jnp.dot(tokens.T, gate_slope, preferred_element_type=jnp.float32)
    up_total = jnp.dot(tokens.T, up_slope, preferred_element_type=jnp.float32)
    down_total = jnp.dot(hidden.T, cotangent, preferred_element_type=jnp.float32)
    return (block_out, input_grad, gate_total.astype(jnp.bfloat16), up_total.astype(jnp.bfloat16), down_total.astype(jnp.bfloat16))
```

```python
import jax
import jax.numpy as jnp
from jax import lax
from jax.sharding import PartitionSpec as P


def contract_last(left_op, right_op):
    return lax.dot_general(
        left_op, right_op, (((1,), (1,)), ((), ())), preferred_element_type=jnp.float32
    )


def contract_first(left_op, right_op):
    return lax.dot_general(
        left_op, right_op, (((0,), (0,)), ((), ())), preferred_element_type=jnp.float32
    )


def gather_block(block):
    wide = lax.all_gather(block, "col", axis=1, tiled=True)
    return lax.all_gather(wide, "tok", axis=0, tiled=True)


def scatter_block(part):
    some = lax.psum_scatter(part, "tok", scatter_dimension=0, tiled=True)
    return lax.psum_scatter(some, "col", scatter_dimension=1, tiled=True).astype(jnp.bfloat16)


def local(tokens, gate_weight, up_weight, down_weight, cotangent):
    features = gather_block(tokens)
    cot = gather_block(cotangent)
    gate_up = jnp.concatenate([gate_weight, up_weight], axis=1)
    parts = jnp.dot(features, gate_up, preferred_element_type=jnp.float32)
    sums = lax.psum_scatter(parts, "row", scatter_dimension=0, tiled=True)
    slope_part = contract_last(cot, down_weight)
    slope = lax.psum_scatter(slope_part, "row", scatter_dimension=0, tiled=True)
    gate_sum, up_sum = jnp.split(sums, 2, axis=1)
    squash = jax.nn.sigmoid(gate_sum)
    swish = gate_sum * squash
    hidden = (swish * up_sum).astype(jnp.bfloat16)
    gate_slope = (slope * up_sum * squash * (1.0 + gate_sum * (1.0 - squash))).astype(jnp.bfloat16)
    up_slope = (slope * swish).astype(jnp.bfloat16)
    hidden = lax.all_gather(hidden, "row", axis=0, tiled=True)
    slopes = jnp.concatenate([gate_slope, up_slope], axis=1)
    slopes = lax.all_gather(slopes, "row", axis=0, tiled=True)
    block_out = scatter_block(jnp.dot(hidden, down_weight, preferred_element_type=jnp.float32))
    input_grad = scatter_block(contract_last(slopes, gate_up))
    grads = contract_first(features, slopes).astype(jnp.bfloat16)
    gate_grad, up_grad = jnp.split(grads, 2, axis=1)
    down_grad = contract_first(hidden, cot).astype(jnp.bfloat16)
    return block_out, input_grad, gate_grad, up_grad, down_grad


def solution(mesh):
    in_specs = (
        P("tok", ("row", "col")),
        P("row", ("col", "tok")),
        P("row", ("col", "tok")),
        P(("col", "tok"), "row"),
        P("tok", ("row", "col")),
    )
    out_specs = (
        P("tok", ("row", "col")),
        P("tok", ("row", "col")),
        P("row", ("col", "tok")),
        P("row", ("col", "tok")),
        P(("col", "tok"), "row"),
    )
    return jax.shard_map(local, mesh=mesh, in_specs=in_specs, out_specs=out_specs, check_vma=False)
```

```python
from types import SimpleNamespace

import math

import jax
import jax.numpy as jnp
from jax import lax
from jax.experimental import pallas as pl
from jax.experimental.pallas import tpu as pltpu
from jax.sharding import PartitionSpec as P

BF, F32 = jnp.bfloat16, jnp.float32
MESH = pl.DeviceIdType.MESH
SENDS = 103
VMEM_LIMIT = 60 * 2 ** 20
POOL = 32


def dot(a, b):
    return jnp.dot(a, b, preferred_element_type=F32)


def dot_t(a, b):
    return lax.dot_general(a, b, (((1,), (1,)), ((), ())), preferred_element_type=F32)


class Scatter:
    NAMES = ("part", "sy3", "yr3", "sy2", "yr2", "sx1", "xr1", "sx2", "xr2", "sb", "br3", "br2",
             "sd", "rd", "fin", "zlr")

    @staticmethod
    def shapes(fs, ct):
        h = fs // 2
        v = pltpu.VMEM
        return [
            v((4, 2, 4, fs, ct), F32),
            v((2, 4, h, ct), BF), v((2, 4, h, ct), BF),
            v((2, 2, 4, h, ct), BF), v((2, 2, 4, h, ct), BF),
            v((4, 2, h, ct), BF), v((4, 2, h, ct), BF),
            v((4, 2, 2, h, ct), BF), v((4, 2, 2, h, ct), BF),
            v((4, 2, h, ct), F32),
            v((2, h, ct), F32), v((2, 2, h, ct), F32),
            v((4, 3, h, ct), BF), v((4, 3, h, ct), BF),
            v((2, fs, ct), F32), v((fs, ct), F32),
        ]

    def __init__(self, refs):
        for name, ref in zip(self.NAMES, refs):
            setattr(self, name, ref)


def kernel(tok_hbm, gw_hbm, uw_hbm, dw_hbm, cot_hbm,
           out_ref, inp_ref, gg_ref, ug_ref, dg_ref, *scratch):
    n_sc = len(Scatter.NAMES)
    (tok_ref, cot_ref, gw, uw, dw, gut, dwt, xt, ct, gu_part, gu_recv, gu_s1, gu_r1, gu_s2, gu_r2,
     sl_part, sl_recv, sl_s1, sl_r1, sl_s2, sl_r2, swish_ref, deriv_ref, hid, slo,
     *rest) = scratch
    so, si = Scatter(rest[:n_sc]), Scatter(rest[n_sc:2 * n_sc])
    grads, most, acts_out, wsem, send_sem, recv_sem = rest[2 * n_sc:]

    y, row, col = lax.axis_index("tok"), lax.axis_index("row"), lax.axis_index("col")
    z, c, zl, x = row // 2, row % 2, col // 4, col % 4
    zo = 1 - zl
    wrap = lambda v: lax.rem(v + 4, 4)
    xp1, xm1, xp2 = wrap(x + 1), wrap(x - 1), wrap(x + 2)
    zp1, zm1, zp2 = wrap(z + 1), wrap(z - 1), wrap(z + 2)
    XP, XM = (y, row, zl * 4 + xp1), (y, row, zl * 4 + xm1)
    X2 = (y, row, zl * 4 + xp2)
    Z2 = (y, zp2 * 2 + c, col)
    YP, YM = (wrap(y + 1), row, col), (wrap(y - 1), row, col)
    ZP, ZM = (y, zp1 * 2 + c, col), (y, zm1 * 2 + c, col)
    ZL, CORE = (y, row, (1 - zl) * 4 + x), (y, z * 2 + 1 - c, col)

    fs = tok_ref.shape[1]
    h = fs // 2
    A, B = pl.ds(0, h), pl.ds(h, h)
    ff = dw.shape[0]
    fq = ff // 4
    depth = gw.shape[0]

    copies, due = [], []

    def fresh():
        due.append(0)
        return len(due) - 1

    def send(src, dst, device, n=None):
        n = fresh() if n is None else n
        m = len(copies)
        if m >= POOL:
            copies[m - POOL].wait_send()
        cp = pltpu.make_async_remote_copy(
            src_ref=src, dst_ref=dst, send_sem=send_sem.at[m % POOL], recv_sem=recv_sem.at[n],
            device_id=device, device_id_type=MESH)
        cp.start()
        copies.append(cp)
        due[n] += math.prod(dst.shape) * dst.dtype.itemsize
        return cp

    def take(n, like):
        assert math.prod(like.shape) * like.dtype.itemsize == due[n]
        pltpu.make_async_remote_copy(
            src_ref=like, dst_ref=like, send_sem=send_sem.at[0], recv_sem=recv_sem.at[n],
            device_id=XP, device_id_type=MESH).wait_recv()

    loads = [pltpu.make_async_copy(s, d, wsem.at[i])
             for i, (s, d) in enumerate((
                 (gw_hbm, gut.at[:, 0]), (uw_hbm, gut.at[:, 1]), (dw_hbm, dw)))]
    acts = [pltpu.make_async_copy(s, d, wsem.at[6 + i])
            for i, (s, d) in enumerate(((tok_hbm, tok_ref), (cot_hbm, cot_ref)))]
    for cp in acts + loads:
        cp.start()
    barrier = pltpu.get_barrier_semaphore()
    for device in (XP, XM, X2, YP, YM, ZP, ZM, Z2, ZL, CORE):
        pl.semaphore_signal(barrier, inc=1, device_id=device, device_id_type=MESH)
    for cp in acts:
        cp.wait()
    xt[0, zl, x] = tok_ref[...].T
    ct[0, zl, x] = cot_ref[...].T
    pl.semaphore_wait(barrier, 10)

    def gather(v):
        k = {}
        gx, g2, gy = fresh(), fresh(), fresh()

        def spread(blk, far2, far1, *yps):
            send(blk, blk, XP, gx)
            send(blk, blk, XM, gx)
            yp = send(blk, far2, YP, *yps)
            send(blk, far1, YM, gy)
            send(blk, blk, X2, g2)
            return yp

        def s0():
            k["zl"] = send(v.at[0, zl, x], v.at[0, zl, x], ZL)
            k["yp"] = spread(v.at[0, zl, x], v.at[2, zl, x], v.at[1, zl, x])

        def s1():
            k["zl"].wait_recv()
            spread(v.at[0, zo, x], v.at[2, zo, x], v.at[1, zo, x], gy)

        def s1y():
            k["yp"].wait_recv()
            k["yf"] = fresh()
            send(v.at[2, zl, x], v.at[3, zl, x], YP, k["yf"])

        def ysend(xi, n):
            blk = v.at[0, :, xi, A]
            send(blk, v.at[2, :, xi, A], YP, n)
            send(blk, v.at[1, :, xi, A], YM, n)

        def s2():
            take(gx, v.at[0, :, pl.ds(0, 2)])
            k["a"] = fresh()
            ysend(xm1, k["a"])
            ysend(xp1, k["a"])

        def xsend(s, n):
            blk = v.at[s, :, x, B]
            send(blk, blk, XP, n)
            send(blk, blk, XM, n)

        def xfwd(s, n):
            send(v.at[s, 0, xm1, B], v.at[s, 0, xm1, B], XP, n)
            send(v.at[s, 1, xp1, B], v.at[s, 1, xp1, B], XM, n)

        def s2b():
            take(gy, v.at[0, 0, pl.ds(0, 3)])
            send(v.at[1, zo, x], v.at[3, zo, x], YM, k["yf"])
            k["x"] = fresh()
            xsend(2, k["x"])
            xsend(1, k["x"])

        def s3():
            take(g2, v.at[0, :, 0])
            ysend(xp2, k["a"])

        def s4():
            take(k["x"], v.at[0, :, pl.ds(0, 2)])
            k["xf"] = fresh()
            xfwd(1, k["xf"])
            xfwd(2, k["xf"])

        def s4b():
            take(k["yf"], v.at[0, :, 0])
            k["x3"] = fresh()
            xsend(3, k["x3"])

        def s5():
            take(k["a"], v.at[0, :, pl.ds(0, 3)])
            k["e"] = fresh()
            for xi in (xm1, xp1, xp2):
                send(v.at[2, 0, xi, A], v.at[3, 0, xi, A], YP, k["e"])
                send(v.at[1, 1, xi, A], v.at[3, 1, xi, A], YM, k["e"])

        def s6():
            take(k["xf"], v.at[0, 0, pl.ds(0, 2)])

        def s7():
            take(k["x3"], v.at[0, :, 0])
            k["xf3"] = fresh()
            xfwd(3, k["xf3"])

        def s8():
            take(k["e"], v.at[0, 0, pl.ds(0, 3)])
            take(k["xf3"], v.at[0, 0, 0])

        return SimpleNamespace(s0=s0, s1=s1, s1y=s1y, s2=s2, s2b=s2b, s3=s3, s4=s4, s4b=s4b, s5=s5, s6=s6, s7=s7, s8=s8)

    def row_sum(compute, finish, part, recv, s1, r1, s2, r2, cut):
        k = {}
        rows = part.shape[3]
        top, low = pl.ds(0, cut), pl.ds(cut, rows - cut)

        def chip(i, q, rs):
            return part[i, c, q, rs] + recv[i, q, rs]

        def a(i):
            total = compute(i)
            part[i, 0] = total[:, :128].reshape(part.shape[2:])
            part[i, 1] = total[:, 128:].reshape(part.shape[2:])
            k["c", i] = send(part.at[i, 1 - c], recv.at[i], CORE)

        def b(i):
            k["c", i].wait_recv()
            s1[i, top] = chip(i, zp2, top).astype(BF)
            s1[i, low] = chip(i, zp2, low).astype(BF)
            k["t", i] = fresh()
            send(s1.at[i, top], r1.at[i, top], ZP, k["t", i])
            send(s1.at[i, low], r1.at[i, low], ZM, k["t", i])

        def cc(i):
            s2[i, 0, low] = chip(i, zp1, low).astype(BF)
            s2[i, 1, top] = chip(i, zm1, top).astype(BF)
            take(k["t", i], r1.at[i])
            k["p", i] = fresh()
            s2[i, 0, top] = (chip(i, zp1, top) + r1[i, top].astype(F32)).astype(BF)
            send(s2.at[i, 0], r2.at[i, 0], ZP, k["p", i])
            s2[i, 1, low] = (chip(i, zm1, low) + r1[i, low].astype(F32)).astype(BF)
            send(s2.at[i, 1], r2.at[i, 1], ZM, k["p", i])

        def d(i):
            take(k["p", i], r2.at[i])
            full = pl.ds(0, rows)
            finish(i, chip(i, z, full) + (r2[i, 0].astype(F32) + r2[i, 1].astype(F32)))

        return SimpleNamespace(a=a, b=b, c=cc, d=d)

    def row_gather(block, first, second, whole, pair, direct=()):
        k = {}

        def a(i):
            k["p", i] = fresh()
            send(block(i, z), block(i, z), ZP, k["p", i])
            send(block(i, z), block(i, z), ZM, k["p", i])
            if i in direct:
                k["f", i] = send(block(i, z), block(i, z), Z2, k["p", i])

        def b(i):
            if i in direct:
                return
            take(k["p", i], pair(i))
            k["f", i] = fresh()
            send(first(i, zm1), first(i, zm1), ZP, k["f", i])
            send(second(i, zp1), second(i, zp1), ZM, k["f", i])

        def cc(i):
            if i in direct:
                take(k["p", i], pair(i, 3))
            else:
                take(k["f", i], block(i, 0))
            k["c", i] = send(whole(i), whole(i), CORE)

        def d(i):
            k["c", i].wait_recv()

        return SimpleNamespace(a=a, b=b, c=cc, d=d)

    def scatter(s, compute, n, ref):
        k = {}
        gy, gb = fresh(), fresh()

        def part(i):
            s.part[i] = compute(i).reshape(s.part.shape[1:])

        def x1(i):
            s.sx1[i] = s.part[i, :, xp2, B].astype(BF)
            k["x1", i] = fresh()
            send(s.sx1.at[i, 0], s.xr1.at[i, 0], XP, k["x1", i])
            send(s.sx1.at[i, 1], s.xr1.at[i, 1], XM, k["x1", i])

        def x2(i):
            take(k["x1", i], s.xr1.at[i])
            k["x2", i] = fresh()
            s.sx2[i, 0, 0] = (s.part[i, 0, xp1, B] + s.xr1[i, 0].astype(F32)).astype(BF)
            s.sx2[i, 0, 1] = s.part[i, 1, xp1, B].astype(BF)
            send(s.sx2.at[i, 0], s.xr2.at[i, 0], XP, k["x2", i])
            s.sx2[i, 1, 0] = s.part[i, 0, xm1, B].astype(BF)
            s.sx2[i, 1, 1] = (s.part[i, 1, xm1, B] + s.xr1[i, 1].astype(F32)).astype(BF)
            send(s.sx2.at[i, 1], s.xr2.at[i, 1], XM, k["x2", i])

        def x3(i):
            take(k["x2", i], s.xr2.at[i])
            s.sb[i] = s.part[i, :, x, B] + (s.xr2[i, 0].astype(F32) + s.xr2[i, 1].astype(F32))

        def y1():
            s.sy3[...] = s.part[3, :, :, A].astype(BF)
            k["y1p"] = send(s.sy3.at[0], s.yr3.at[0], YP)
            k["y1m"] = send(s.sy3.at[1], s.yr3.at[1], YM)

        def y2p():
            s.sy2[0, 1] = s.part[1, 1, :, A].astype(BF)
            k["y1p"].wait_recv()
            s.sy2[0, 0] = (s.part[1, 0, :, A] + s.yr3[0].astype(F32)).astype(BF)
            send(s.sy2.at[0], s.yr2.at[0], YP, gy)

        def y2m():
            s.sy2[1, 0] = s.part[2, 0, :, A].astype(BF)
            k["y1m"].wait_recv()
            s.sy2[1, 1] = (s.part[2, 1, :, A] + s.yr3[1].astype(F32)).astype(BF)
            send(s.sy2.at[1], s.yr2.at[1], YM, gy)

        def xsend(name, n, blk):
            k[name] = fresh()
            for d, (xi, device) in enumerate(((xp1, XP), (xm1, XM), (xp2, X2))):
                s.sd[n, d] = blk(xi).astype(BF)
                send(s.sd.at[n, d], s.rd.at[n, d], device, k[name])

        def xtake(name, n, blk):
            take(k[name], s.rd.at[n])
            return blk(x) + (s.rd[n, 0].astype(F32) + s.rd[n, 1].astype(F32) + s.rd[n, 2].astype(F32))

        def ablk(p):
            return lambda xi: s.part[0, p, xi, A] + (s.yr2[0, p, xi].astype(F32) + s.yr2[1, p, xi].astype(F32))

        def cblk(p):
            return lambda xi: s.part[0, p, xi, B]

        def a1q():
            take(gy, s.yr2)
            xsend("aq", 0, ablk(zo))

        def a1o():
            xsend("ao", 1, ablk(zl))

        def c1q():
            xsend("cq", 2, cblk(zo))

        def c1o():
            xsend("co", 3, cblk(zl))

        def a3q():
            s.fin[zo, A] = xtake("aq", 0, ablk(zo))

        def a3o():
            s.fin[zl, A] = xtake("ao", 1, ablk(zl))

        def c3q():
            s.fin[zo, B] = xtake("cq", 2, cblk(zo)) + (s.br2[0, zo] + s.br2[1, zo])

        def c3o():
            s.fin[zl, B] = xtake("co", 3, cblk(zl)) + (s.br2[0, zl] + s.br2[1, zl])

        def b1():
            k["b1"] = fresh()
            send(s.sb.at[3, 0], s.br3.at[0], YP, k["b1"])
            send(s.sb.at[3, 1], s.br3.at[1], YM, k["b1"])

        def b2():
            take(k["b1"], s.br3)
            s.sb[1, 0] = s.sb[1, 0] + s.br3[0]
            send(s.sb.at[1], s.br2.at[0], YP, gb)
            s.sb[2, 1] = s.sb[2, 1] + s.br3[1]
            send(s.sb.at[2], s.br2.at[1], YM, gb)

        def b3():
            take(gb, s.br2)

        def f1():
            k["f"] = send(s.fin.at[zo], s.zlr, ZL)

        def f2():
            k["f"].wait_recv()
            acts_out[n] = (s.fin[zl] + s.zlr[...]).T.astype(BF)
            cp = pltpu.make_async_copy(acts_out.at[n], ref, wsem.at[8 + n])
            cp.start()
            loads.append(cp)

        return SimpleNamespace(part=part, x1=x1, x2=x2, x3=x3, y1=y1, y2p=y2p, y2m=y2m, a1q=a1q, a1o=a1o,
                    a3q=a3q, a3o=a3o, c1q=c1q, c1o=c1o, c3q=c3q, c3o=c3o,
                    b1=b1, b2=b2, b3=b3, f1=f1, f2=f2)

    def chunk(v, i):
        return v[i].reshape(depth, v.shape[-1])

    def act(i, total):
        gate, up = total[:fq], total[fq:]
        squash = 1.0 / (1.0 + jnp.exp(-gate))
        swish = gate * squash
        swish_ref[i] = swish
        deriv_ref[i] = up * squash * (1.0 + gate * (1.0 - squash))
        hid[i, c, z] = (swish * up).astype(BF)

    def slopes(i, total):
        slo[i, c, 0, z] = (total * deriv_ref[i]).astype(BF)
        slo[i, c, 1, z] = (total * swish_ref[i]).astype(BF)

    def hidden_of(i):
        return jnp.concatenate([hid[i, j].reshape(ff, 128) for j in range(2)], axis=1)

    def slope_of(i, g):
        return jnp.concatenate([slo[i, j, g].reshape(ff, 128) for j in range(2)], axis=1)

    X, C = gather(xt), gather(ct)
    GU = row_sum(lambda i: dot(gut[...].reshape(2 * ff, depth), chunk(xt, i)), act,
                 gu_part, gu_recv, gu_s1, gu_r1, gu_s2, gu_r2, fq)
    S = row_sum(lambda i: dot(dw[...], chunk(ct, i)), slopes,
                sl_part, sl_recv, sl_s1, sl_r1, sl_s2, sl_r2, 64)
    H = row_gather(lambda i, q: hid.at[i, c, q],
                   lambda i, q: hid.at[i, c, q, pl.ds(0, 64)],
                   lambda i, q: hid.at[i, c, q, pl.ds(64, fq - 64)],
                   lambda i: hid.at[i, c], lambda i, n=2: hid.at[i, c, pl.ds(0, n)])
    G = row_gather(lambda i, q: slo.at[i, c, :, q],
                   lambda i, q: slo.at[i, c, 0, q],
                   lambda i, q: slo.at[i, c, 1, q],
                   lambda i: slo.at[i, c], lambda i, n=2: slo.at[i, c, :, pl.ds(0, n)], (0,))
    O = scatter(so, lambda i: dot(dwt[...], hidden_of(i)), 0, out_ref)
    I = scatter(si, lambda i: dot(gw[...], slope_of(i, 0)) + dot(uw[...], slope_of(i, 1)), 1, inp_ref)

    def wait_gate_up():
        for cp in loads[:2]:
            cp.wait()

    def turn_gate_up():
        for g, w in enumerate((gw, uw)):
            w[...] = gut[:, g].reshape(ff, depth).T

    def turn_down():
        loads[2].wait()
        dwt[...] = dw[...].T

    def leave(n, ref):
        cp = pltpu.make_async_copy(grads.at[n], ref, wsem.at[3 + n])
        cp.start()
        loads.append(cp)

    def down_grad():
        total = dot_t(hidden_of(0), chunk(ct, 0))
        for i in range(1, 4):
            total += dot_t(hidden_of(i), chunk(ct, i))
        grads[2] = total.astype(BF)
        leave(2, dg_ref)

    def most_grad(g):
        total = dot_t(slope_of(3, g), chunk(xt, 3))
        for i in (2, 1):
            total += dot_t(slope_of(i, g), chunk(xt, i))
        most[g] = total

    def weight_grad(ref, g):
        grads[g] = (most[g] + dot_t(slope_of(0, g), chunk(xt, 0))).astype(BF)
        leave(g, ref)

    X.s0(); wait_gate_up(); turn_gate_up(); turn_down(); X.s1(); X.s1y(); X.s2b(); X.s2(); X.s3(); C.s0()
    GU.a(0); GU.b(0); X.s4(); X.s4b(); C.s1(); C.s1y(); X.s5(); GU.c(0); X.s6(); GU.a(2); X.s7(); C.s2b()
    GU.a(1); GU.b(2); C.s2(); C.s3(); X.s8(); GU.b(1); GU.d(0); C.s4b(); H.a(0); GU.a(3); GU.c(2); C.s4()
    GU.b(3); GU.c(1); C.s7(); C.s5(); H.b(0); C.s6(); S.a(1); S.a(2); GU.d(2); GU.c(3); S.b(2); C.s8()
    H.a(2); S.a(3); H.c(0); S.b(3); H.d(0); S.b(1); O.part(0); GU.d(3); H.a(3); GU.d(1); H.a(1); O.c1o()
    S.c(3); H.b(2); H.b(3); S.c(2); S.a(0); O.c1q(); S.c(1); S.d(3); G.a(3); H.b(1); H.c(2); H.c(3); H.d(2)
    S.d(2); G.a(2); H.d(3); O.part(3); O.x1(3); O.y1(); O.part(2); O.x1(2); G.b(3); S.b(0); O.x2(3); H.c(1)
    S.d(1); G.a(1); O.x2(2); H.d(1); O.part(1); O.y2p(); O.y2m(); G.c(3); O.x3(3); G.b(2); S.c(0); O.x1(1)
    G.d(3); I.part(3); I.x1(3); G.b(1); O.x3(2); I.y1(); O.x2(1); G.c(2); O.b1(); I.x2(3); S.d(0); G.a(0)
    G.d(2); G.c(1); I.part(2); I.x1(2); G.d(1); I.part(1); I.x3(3); I.b1(); I.y2p(); O.x3(1); I.y2m()
    I.x1(1); O.a1q(); I.x2(2); most_grad(0); O.b2(); G.b(0); I.x2(1); G.c(0); O.a1o(); G.d(0); I.part(0)
    I.c1q(); I.x3(2); O.a3q(); I.x3(1); I.b2(); I.a1q(); weight_grad(gg_ref, 0); I.c1o(); I.a1o(); O.a3o()
    O.b3(); O.c3q(); O.f1(); most_grad(1); O.c3o(); I.a3q(); I.b3(); I.c3q(); I.f1(); I.c3o(); down_grad()
    weight_grad(ug_ref, 1); I.a3o(); O.f2(); I.f2()
    for cp in copies[-POOL:]:
        cp.wait_send()
    for cp in loads[3:]:
        cp.wait()


def publish_kernel(*refs):
    n = (len(refs) - 2) // 3
    src, dst, mid, (isem, osem) = refs[:n], refs[n:2 * n], refs[2 * n:3 * n], refs[3 * n:]
    ins = [pltpu.make_async_copy(src[i], mid[i], isem.at[i]) for i in range(n)]
    outs = [pltpu.make_async_copy(mid[i], dst[i], osem.at[i]) for i in range(n)]
    for cp in ins:
        cp.start()
    for cp, out in zip(ins, outs):
        cp.wait()
        out.start()
    for out in outs:
        out.wait()


def publish(arrays):
    n = len(arrays)
    hbm = pl.BlockSpec(memory_space=pltpu.HBM)
    sem = pltpu.SemaphoreType.DMA((n,))
    return pl.pallas_call(
        publish_kernel,
        out_shape=[jax.ShapeDtypeStruct(a.shape, a.dtype) for a in arrays],
        in_specs=[hbm] * n,
        out_specs=[hbm] * n,
        scratch_shapes=[*(pltpu.VMEM(a.shape, a.dtype) for a in arrays), sem, sem],
        compiler_params=pltpu.CompilerParams(vmem_limit_bytes=VMEM_LIMIT),
    )(*arrays)


def local(tokens, gate_weight, up_weight, down_weight, cotangent):
    ct, fs = tokens.shape
    depth, ff = gate_weight.shape
    fq = ff // 4
    v = pltpu.VMEM
    scratch = [
        v((ct, fs), BF), v((ct, fs), BF),
        v((depth, ff), BF), v((depth, ff), BF), v((ff, depth), BF),
        v((4, 2, fq, depth), BF), v((depth, ff), BF),
        v((4, 2, 4, fs, ct), BF), v((4, 2, 4, fs, ct), BF),
        v((4, 2, 4, 2 * fq, 128), F32), v((4, 4, 2 * fq, 128), F32),
        v((4, 2 * fq, 128), BF), v((4, 2 * fq, 128), BF),
        v((4, 2, 2 * fq, 128), BF), v((4, 2, 2 * fq, 128), BF),
        v((4, 2, 4, fq, 128), F32), v((4, 4, fq, 128), F32),
        v((4, fq, 128), BF), v((4, fq, 128), BF),
        v((4, 2, fq, 128), BF), v((4, 2, fq, 128), BF),
        v((4, fq, 128), F32), v((4, fq, 128), F32),
        v((4, 2, 4, fq, 128), BF), v((4, 2, 2, 4, fq, 128), BF),
        *Scatter.shapes(fs, ct), *Scatter.shapes(fs, ct),
        v((3, ff, depth), BF), v((2, ff, depth), F32), v((2, ct, fs), BF),
        pltpu.SemaphoreType.DMA((10,)),
        pltpu.SemaphoreType.DMA((POOL,)), pltpu.SemaphoreType.DMA((SENDS,)),
    ]
    hbm = pl.BlockSpec(memory_space=pltpu.HBM)
    sds = jax.ShapeDtypeStruct
    results = pl.pallas_call(
        kernel,
        out_shape=[sds((ct, fs), BF), sds((ct, fs), BF), sds((ff, depth), BF),
                   sds((ff, depth), BF), sds((ff, depth), BF)],
        in_specs=[hbm] * 5,
        out_specs=[hbm] * 5,
        scratch_shapes=scratch,
        compiler_params=pltpu.CompilerParams(
            collective_id=0, has_side_effects=True, vmem_limit_bytes=VMEM_LIMIT),
    )(tokens, gate_weight.T.reshape(4, fq, depth), up_weight.T.reshape(4, fq, depth), down_weight, cotangent)
    block_out, input_grad, gate_grad, up_grad, down_grad = publish(results)
    return block_out, input_grad, gate_grad.T, up_grad.T, down_grad


def solution(mesh):
    in_specs = (
        P("tok", ("row", "col")),
        P("row", ("col", "tok")),
        P("row", ("col", "tok")),
        P(("col", "tok"), "row"),
        P("tok", ("row", "col")),
    )
    out_specs = (
        P("tok", ("row", "col")),
        P("tok", ("row", "col")),
        P("row", ("col", "tok")),
        P("row", ("col", "tok")),
        P(("col", "tok"), "row"),
    )
    return jax.shard_map(local, mesh=mesh, in_specs=in_specs, out_specs=out_specs, check_vma=False)
```

```python
from types import SimpleNamespace

import math

import jax
import jax.numpy as jnp
from jax import lax
from jax.experimental import pallas as pl
from jax.experimental.pallas import tpu as pltpu
from jax.sharding import PartitionSpec as P

BF, F32 = jnp.bfloat16, jnp.float32
MESH = pl.DeviceIdType.MESH
SENDS = 103
VMEM_LIMIT = 60 * 2 ** 20
POOL = 32


def dot(a, b):
    return jnp.dot(a, b, preferred_element_type=F32)


def dot_t(a, b):
    return lax.dot_general(a, b, (((1,), (1,)), ((), ())), preferred_element_type=F32)


class Scatter:
    NAMES = ("part", "sy3", "yr3", "sy2", "yr2", "sx1", "xr1", "sx2", "xr2", "sb", "br3", "br2",
             "sd", "rd", "fin", "zlr")

    @staticmethod
    def shapes(fs, ct):
        h = fs // 2
        v = pltpu.VMEM
        return [
            v((4, 2, 4, fs, ct), F32),
            v((2, 4, h, ct), BF), v((2, 4, h, ct), BF),
            v((2, 2, 4, h, ct), BF), v((2, 2, 4, h, ct), BF),
            v((4, 2, h, ct), BF), v((4, 2, h, ct), BF),
            v((4, 2, 2, h, ct), BF), v((4, 2, 2, h, ct), BF),
            v((4, 2, h, ct), F32),
            v((2, h, ct), F32), v((2, 2, h, ct), F32),
            v((4, 3, h, ct), BF), v((4, 3, h, ct), BF),
            v((2, fs, ct), F32), v((fs, ct), F32),
        ]

    def __init__(self, refs):
        for name, ref in zip(self.NAMES, refs):
            setattr(self, name, ref)


def kernel(tok_hbm, gw_hbm, uw_hbm, dw_hbm, cot_hbm,
           out_ref, inp_ref, gg_ref, ug_ref, dg_ref, *scratch):
    n_sc = len(Scatter.NAMES)
    (tok_ref, cot_ref, gw, uw, dw, gut, dwt, xt, ct, gu_part, gu_recv, gu_s1, gu_r1, gu_s2, gu_r2,
     sl_part, sl_recv, sl_s1, sl_r1, sl_s2, sl_r2, swish_ref, deriv_ref, hid, slo,
     *rest) = scratch
    so, si = Scatter(rest[:n_sc]), Scatter(rest[n_sc:2 * n_sc])
    grads, most, acts_out, wsem, send_sem, recv_sem = rest[2 * n_sc:]

    y, row, col = lax.axis_index("tok"), lax.axis_index("row"), lax.axis_index("col")
    z, c, zl, x = row // 2, row % 2, col // 4, col % 4
    zo = 1 - zl
    wrap = lambda v: lax.rem(v + 4, 4)
    xp1, xm1, xp2 = wrap(x + 1), wrap(x - 1), wrap(x + 2)
    zp1, zm1, zp2 = wrap(z + 1), wrap(z - 1), wrap(z + 2)
    XP, XM = (y, row, zl * 4 + xp1), (y, row, zl * 4 + xm1)
    X2 = (y, row, zl * 4 + xp2)
    Z2 = (y, zp2 * 2 + c, col)
    YP, YM = (wrap(y + 1), row, col), (wrap(y - 1), row, col)
    ZP, ZM = (y, zp1 * 2 + c, col), (y, zm1 * 2 + c, col)
    ZL, CORE = (y, row, (1 - zl) * 4 + x), (y, z * 2 + 1 - c, col)

    fs = tok_ref.shape[1]
    h = fs // 2
    A, B = pl.ds(0, h), pl.ds(h, h)
    ff = dw.shape[0]
    fq = ff // 4
    depth = gw.shape[0]

    copies, due = [], []

    def fresh():
        due.append(0)
        return len(due) - 1

    def send(src, dst, device, n=None):
        n = fresh() if n is None else n
        m = len(copies)
        if m >= POOL:
            copies[m - POOL].wait_send()
        cp = pltpu.make_async_remote_copy(
            src_ref=src, dst_ref=dst, send_sem=send_sem.at[m % POOL], recv_sem=recv_sem.at[n],
            device_id=device, device_id_type=MESH)
        cp.start()
        copies.append(cp)
        due[n] += math.prod(dst.shape) * dst.dtype.itemsize
        return cp

    def take(n, like):
        assert math.prod(like.shape) * like.dtype.itemsize == due[n]
        pltpu.make_async_remote_copy(
            src_ref=like, dst_ref=like, send_sem=send_sem.at[0], recv_sem=recv_sem.at[n],
            device_id=XP, device_id_type=MESH).wait_recv()

    loads = [pltpu.make_async_copy(s, d, wsem.at[i])
             for i, (s, d) in enumerate((
                 (gw_hbm, gut.at[:, 0]), (uw_hbm, gut.at[:, 1]), (dw_hbm, dw)))]
    acts = [pltpu.make_async_copy(s, d, wsem.at[6 + i])
            for i, (s, d) in enumerate(((tok_hbm, tok_ref), (cot_hbm, cot_ref)))]
    for cp in acts + loads:
        cp.start()
    barrier = pltpu.get_barrier_semaphore()
    for device in (XP, XM, X2, YP, YM, ZP, ZM, Z2, ZL, CORE):
        pl.semaphore_signal(barrier, inc=1, device_id=device, device_id_type=MESH)
    for cp in acts:
        cp.wait()
    xt[0, zl, x] = tok_ref[...].T
    ct[0, zl, x] = cot_ref[...].T
    pl.semaphore_wait(barrier, 10)

    def gather(v):
        k = {}
        gx, g2, gy = fresh(), fresh(), fresh()

        def spread(blk, far2, far1, *yps):
            send(blk, blk, XP, gx)
            send(blk, blk, XM, gx)
            yp = send(blk, far2, YP, *yps)
            send(blk, far1, YM, gy)
            send(blk, blk, X2, g2)
            return yp

        def s0():
            k["zl"] = send(v.at[0, zl, x], v.at[0, zl, x], ZL)
            k["yp"] = spread(v.at[0, zl, x], v.at[2, zl, x], v.at[1, zl, x])

        def s1():
            k["zl"].wait_recv()
            spread(v.at[0, zo, x], v.at[2, zo, x], v.at[1, zo, x], gy)

        def s1y():
            k["yp"].wait_recv()
            k["yf"] = fresh()
            send(v.at[2, zl, x], v.at[3, zl, x], YP, k["yf"])

        def ysend(xi, n):
            blk = v.at[0, :, xi, A]
            send(blk, v.at[2, :, xi, A], YP, n)
            send(blk, v.at[1, :, xi, A], YM, n)

        def s2():
            take(gx, v.at[0, :, pl.ds(0, 2)])
            k["a"] = fresh()
            ysend(xm1, k["a"])
            ysend(xp1, k["a"])

        def xsend(s, n):
            blk = v.at[s, :, x, B]
            send(blk, blk, XP, n)
            send(blk, blk, XM, n)

        def xfwd(s, n):
            send(v.at[s, 0, xm1, B], v.at[s, 0, xm1, B], XP, n)
            send(v.at[s, 1, xp1, B], v.at[s, 1, xp1, B], XM, n)

        def s2b():
            take(gy, v.at[0, 0, pl.ds(0, 3)])
            send(v.at[1, zo, x], v.at[3, zo, x], YM, k["yf"])
            k["x"] = fresh()
            xsend(2, k["x"])
            xsend(1, k["x"])

        def s3():
            take(g2, v.at[0, :, 0])
            ysend(xp2, k["a"])

        def s4():
            take(k["x"], v.at[0, :, pl.ds(0, 2)])
            k["xf"] = fresh()
            xfwd(1, k["xf"])
            xfwd(2, k["xf"])

        def s4b():
            take(k["yf"], v.at[0, :, 0])
            k["x3"] = fresh()
            xsend(3, k["x3"])

        def s5():
            take(k["a"], v.at[0, :, pl.ds(0, 3)])
            k["e"] = fresh()
            for xi in (xm1, xp1, xp2):
                send(v.at[2, 0, xi, A], v.at[3, 0, xi, A], YP, k["e"])
                send(v.at[1, 1, xi, A], v.at[3, 1, xi, A], YM, k["e"])

        def s6():
            take(k["xf"], v.at[0, 0, pl.ds(0, 2)])

        def s7():
            take(k["x3"], v.at[0, :, 0])
            k["xf3"] = fresh()
            xfwd(3, k["xf3"])

        def s8():
            take(k["e"], v.at[0, 0, pl.ds(0, 3)])
            take(k["xf3"], v.at[0, 0, 0])

        return SimpleNamespace(s0=s0, s1=s1, s1y=s1y, s2=s2, s2b=s2b, s3=s3, s4=s4, s4b=s4b, s5=s5, s6=s6, s7=s7, s8=s8)

    def row_sum(compute, finish, part, recv, s1, r1, s2, r2, cut):
        k = {}
        rows = part.shape[3]
        top, low = pl.ds(0, cut), pl.ds(cut, rows - cut)

        def chip(i, q, rs):
            return part[i, c, q, rs] + recv[i, q, rs]

        def a(i):
            total = compute(i)
            part[i, 0] = total[:, :128].reshape(part.shape[2:])
            part[i, 1] = total[:, 128:].reshape(part.shape[2:])
            k["c", i] = send(part.at[i, 1 - c], recv.at[i], CORE)

        def b(i):
            k["c", i].wait_recv()
            s1[i, top] = chip(i, zp2, top).astype(BF)
            s1[i, low] = chip(i, zp2, low).astype(BF)
            k["t", i] = fresh()
            send(s1.at[i, top], r1.at[i, top], ZP, k["t", i])
            send(s1.at[i, low], r1.at[i, low], ZM, k["t", i])

        def cc(i):
            s2[i, 0, low] = chip(i, zp1, low).astype(BF)
            s2[i, 1, top] = chip(i, zm1, top).astype(BF)
            take(k["t", i], r1.at[i])
            k["p", i] = fresh()
            s2[i, 0, top] = (chip(i, zp1, top) + r1[i, top].astype(F32)).astype(BF)
            send(s2.at[i, 0], r2.at[i, 0], ZP, k["p", i])
            s2[i, 1, low] = (chip(i, zm1, low) + r1[i, low].astype(F32)).astype(BF)
            send(s2.at[i, 1], r2.at[i, 1], ZM, k["p", i])

        def d(i):
            take(k["p", i], r2.at[i])
            full = pl.ds(0, rows)
            finish(i, chip(i, z, full) + (r2[i, 0].astype(F32) + r2[i, 1].astype(F32)))

        return SimpleNamespace(a=a, b=b, c=cc, d=d)

    def row_gather(block, first, second, whole, pair, direct=()):
        k = {}

        def a(i):
            k["p", i] = fresh()
            send(block(i, z), block(i, z), ZP, k["p", i])
            send(block(i, z), block(i, z), ZM, k["p", i])
            if i in direct:
                k["f", i] = send(block(i, z), block(i, z), Z2, k["p", i])

        def b(i):
            if i in direct:
                return
            take(k["p", i], pair(i))
            k["f", i] = fresh()
            send(first(i, zm1), first(i, zm1), ZP, k["f", i])
            send(second(i, zp1), second(i, zp1), ZM, k["f", i])

        def cc(i):
            if i in direct:
                take(k["p", i], pair(i, 3))
            else:
                take(k["f", i], block(i, 0))
            k["c", i] = send(whole(i), whole(i), CORE)

        def d(i):
            k["c", i].wait_recv()

        return SimpleNamespace(a=a, b=b, c=cc, d=d)

    def scatter(s, compute, n, ref):
        k = {}
        gy, gb = fresh(), fresh()

        def part(i):
            s.part[i] = compute(i).reshape(s.part.shape[1:])

        def x1(i):
            s.sx1[i] = s.part[i, :, xp2, B].astype(BF)
            k["x1", i] = fresh()
            send(s.sx1.at[i, 0], s.xr1.at[i, 0], XP, k["x1", i])
            send(s.sx1.at[i, 1], s.xr1.at[i, 1], XM, k["x1", i])

        def x2(i):
            take(k["x1", i], s.xr1.at[i])
            k["x2", i] = fresh()
            s.sx2[i, 0, 0] = (s.part[i, 0, xp1, B] + s.xr1[i, 0].astype(F32)).astype(BF)
            s.sx2[i, 0, 1] = s.part[i, 1, xp1, B].astype(BF)
            send(s.sx2.at[i, 0], s.xr2.at[i, 0], XP, k["x2", i])
            s.sx2[i, 1, 0] = s.part[i, 0, xm1, B].astype(BF)
            s.sx2[i, 1, 1] = (s.part[i, 1, xm1, B] + s.xr1[i, 1].astype(F32)).astype(BF)
            send(s.sx2.at[i, 1], s.xr2.at[i, 1], XM, k["x2", i])

        def x3(i):
            take(k["x2", i], s.xr2.at[i])
            s.sb[i] = s.part[i, :, x, B] + (s.xr2[i, 0].astype(F32) + s.xr2[i, 1].astype(F32))

        def y1():
            s.sy3[...] = s.part[3, :, :, A].astype(BF)
            k["y1p"] = send(s.sy3.at[0], s.yr3.at[0], YP)
            k["y1m"] = send(s.sy3.at[1], s.yr3.at[1], YM)

        def y2p():
            s.sy2[0, 1] = s.part[1, 1, :, A].astype(BF)
            k["y1p"].wait_recv()
            s.sy2[0, 0] = (s.part[1, 0, :, A] + s.yr3[0].astype(F32)).astype(BF)
            send(s.sy2.at[0], s.yr2.at[0], YP, gy)

        def y2m():
            s.sy2[1, 0] = s.part[2, 0, :, A].astype(BF)
            k["y1m"].wait_recv()
            s.sy2[1, 1] = (s.part[2, 1, :, A] + s.yr3[1].astype(F32)).astype(BF)
            send(s.sy2.at[1], s.yr2.at[1], YM, gy)

        def xsend(name, n, blk):
            k[name] = fresh()
            for d, (xi, device) in enumerate(((xp1, XP), (xm1, XM), (xp2, X2))):
                s.sd[n, d] = blk(xi).astype(BF)
                send(s.sd.at[n, d], s.rd.at[n, d], device, k[name])

        def xtake(name, n, blk):
            take(k[name], s.rd.at[n])
            return blk(x) + (s.rd[n, 0].astype(F32) + s.rd[n, 1].astype(F32) + s.rd[n, 2].astype(F32))

        def ablk(p):
            return lambda xi: s.part[0, p, xi, A] + (s.yr2[0, p, xi].astype(F32) + s.yr2[1, p, xi].astype(F32))

        def cblk(p):
            return lambda xi: s.part[0, p, xi, B]

        def a1q():
            take(gy, s.yr2)
            xsend("aq", 0, ablk(zo))

        def a1o():
            xsend("ao", 1, ablk(zl))

        def c1q():
            xsend("cq", 2, cblk(zo))

        def c1o():
            xsend("co", 3, cblk(zl))

        def a3q():
            s.fin[zo, A] = xtake("aq", 0, ablk(zo))

        def a3o():
            s.fin[zl, A] = xtake("ao", 1, ablk(zl))

        def c3q():
            s.fin[zo, B] = xtake("cq", 2, cblk(zo)) + (s.br2[0, zo] + s.br2[1, zo])

        def c3o():
            s.fin[zl, B] = xtake("co", 3, cblk(zl)) + (s.br2[0, zl] + s.br2[1, zl])

        def b1():
            k["b1"] = fresh()
            send(s.sb.at[3, 0], s.br3.at[0], YP, k["b1"])
            send(s.sb.at[3, 1], s.br3.at[1], YM, k["b1"])

        def b2():
            take(k["b1"], s.br3)
            s.sb[1, 0] = s.sb[1, 0] + s.br3[0]
            send(s.sb.at[1], s.br2.at[0], YP, gb)
            s.sb[2, 1] = s.sb[2, 1] + s.br3[1]
            send(s.sb.at[2], s.br2.at[1], YM, gb)

        def b3():
            take(gb, s.br2)

        def f1():
            k["f"] = send(s.fin.at[zo], s.zlr, ZL)

        def f2():
            k["f"].wait_recv()
            acts_out[n] = (s.fin[zl] + s.zlr[...]).T.astype(BF)
            cp = pltpu.make_async_copy(acts_out.at[n], ref, wsem.at[8 + n])
            cp.start()
            loads.append(cp)

        return SimpleNamespace(part=part, x1=x1, x2=x2, x3=x3, y1=y1, y2p=y2p, y2m=y2m, a1q=a1q, a1o=a1o,
                    a3q=a3q, a3o=a3o, c1q=c1q, c1o=c1o, c3q=c3q, c3o=c3o,
                    b1=b1, b2=b2, b3=b3, f1=f1, f2=f2)

    def chunk(v, i):
        return v[i].reshape(depth, v.shape[-1])

    def act(i, total):
        gate, up = total[:fq], total[fq:]
        squash = 1.0 / (1.0 + jnp.exp(-gate))
        swish = gate * squash
        swish_ref[i] = swish
        deriv_ref[i] = up * squash * (1.0 + gate * (1.0 - squash))
        hid[i, c, z] = (swish * up).astype(BF)

    def slopes(i, total):
        slo[i, c, 0, z] = (total * deriv_ref[i]).astype(BF)
        slo[i, c, 1, z] = (total * swish_ref[i]).astype(BF)

    def hidden_of(i):
        return jnp.concatenate([hid[i, j].reshape(ff, 128) for j in range(2)], axis=1)

    def slope_of(i, g):
        return jnp.concatenate([slo[i, j, g].reshape(ff, 128) for j in range(2)], axis=1)

    X, C = gather(xt), gather(ct)
    GU = row_sum(lambda i: dot(gut[...].reshape(2 * ff, depth), chunk(xt, i)), act,
                 gu_part, gu_recv, gu_s1, gu_r1, gu_s2, gu_r2, fq)
    S = row_sum(lambda i: dot(dw[...], chunk(ct, i)), slopes,
                sl_part, sl_recv, sl_s1, sl_r1, sl_s2, sl_r2, 64)
    H = row_gather(lambda i, q: hid.at[i, c, q],
                   lambda i, q: hid.at[i, c, q, pl.ds(0, 64)],
                   lambda i, q: hid.at[i, c, q, pl.ds(64, fq - 64)],
                   lambda i: hid.at[i, c], lambda i, n=2: hid.at[i, c, pl.ds(0, n)])
    G = row_gather(lambda i, q: slo.at[i, c, :, q],
                   lambda i, q: slo.at[i, c, 0, q],
                   lambda i, q: slo.at[i, c, 1, q],
                   lambda i: slo.at[i, c], lambda i, n=2: slo.at[i, c, :, pl.ds(0, n)], (0,))
    O = scatter(so, lambda i: dot(dwt[...], hidden_of(i)), 0, out_ref)
    I = scatter(si, lambda i: dot(gw[...], slope_of(i, 0)) + dot(uw[...], slope_of(i, 1)), 1, inp_ref)

    def wait_gate_up():
        for cp in loads[:2]:
            cp.wait()

    def turn_gate_up():
        for g, w in enumerate((gw, uw)):
            w[...] = gut[:, g].reshape(ff, depth).T

    def turn_down():
        loads[2].wait()
        dwt[...] = dw[...].T

    def leave(n, ref):
        cp = pltpu.make_async_copy(grads.at[n], ref, wsem.at[3 + n])
        cp.start()
        loads.append(cp)

    def down_grad():
        total = dot_t(hidden_of(0), chunk(ct, 0))
        for i in range(1, 4):
            total += dot_t(hidden_of(i), chunk(ct, i))
        grads[2] = total.astype(BF)
        leave(2, dg_ref)

    def most_grad(g):
        total = dot_t(slope_of(3, g), chunk(xt, 3))
        for i in (2, 1):
            total += dot_t(slope_of(i, g), chunk(xt, i))
        most[g] = total

    def weight_grad(ref, g):
        grads[g] = (most[g] + dot_t(slope_of(0, g), chunk(xt, 0))).astype(BF)
        leave(g, ref)

    X.s0(); wait_gate_up(); turn_gate_up(); turn_down(); X.s1(); X.s1y(); X.s2b(); X.s2(); X.s3(); C.s0()
    GU.a(0); GU.b(0); X.s4(); X.s4b(); C.s1(); C.s1y(); X.s5(); GU.c(0); X.s6(); GU.a(2); X.s7(); C.s2b()
    GU.a(1); GU.b(2); C.s2(); C.s3(); X.s8(); GU.b(1); GU.d(0); C.s4b(); H.a(0); GU.a(3); GU.c(2); C.s4()
    GU.b(3); GU.c(1); C.s7(); C.s5(); H.b(0); C.s6(); S.a(1); S.a(2); GU.d(2); GU.c(3); S.b(2); C.s8()
    H.a(2); S.a(3); H.c(0); S.b(3); H.d(0); S.b(1); O.part(0); GU.d(3); H.a(3); GU.d(1); H.a(1); O.c1o()
    S.c(3); H.b(2); H.b(3); S.c(2); S.c(1); S.a(0); O.c1q(); S.d(3); G.a(3); H.b(1); H.c(2); H.c(3); H.d(2)
    S.d(2); G.a(2); H.d(3); O.part(3); O.x1(3); O.y1(); O.part(2); O.x1(2); G.b(3); S.b(0); O.x2(3); H.c(1)
    S.d(1); G.a(1); O.x2(2); H.d(1); O.part(1); O.y2p(); O.y2m(); G.c(3); O.x3(3); G.b(2); S.c(0); O.x1(1)
    G.d(3); I.part(3); I.x1(3); G.b(1); O.x3(2); I.y1(); O.x2(1); G.c(2); O.b1(); I.x2(3); S.d(0); G.a(0)
    G.d(2); G.c(1); I.part(2); I.x1(2); G.d(1); I.part(1); I.x3(3); I.b1(); I.y2p(); O.x3(1); I.y2m()
    I.x1(1); O.a1q(); I.x2(2); most_grad(0); O.b2(); G.b(0); I.x2(1); G.c(0); O.a1o(); G.d(0); I.part(0)
    I.c1q(); I.x3(2); O.a3q(); I.x3(1); I.b2(); I.a1q(); weight_grad(gg_ref, 0); I.c1o(); I.a1o(); O.a3o()
    O.b3(); O.c3q(); O.f1(); most_grad(1); O.c3o(); I.a3q(); I.b3(); I.c3q(); I.f1(); I.c3o(); down_grad()
    weight_grad(ug_ref, 1); I.a3o(); O.f2(); I.f2()
    for cp in copies[-POOL:]:
        cp.wait_send()
    for cp in loads[3:]:
        cp.wait()


def publish_kernel(*refs):
    n = (len(refs) - 2) // 3
    src, dst, mid, (isem, osem) = refs[:n], refs[n:2 * n], refs[2 * n:3 * n], refs[3 * n:]
    ins = [pltpu.make_async_copy(src[i], mid[i], isem.at[i]) for i in range(n)]
    outs = [pltpu.make_async_copy(mid[i], dst[i], osem.at[i]) for i in range(n)]
    for cp in ins:
        cp.start()
    for cp, out in zip(ins, outs):
        cp.wait()
        out.start()
    for out in outs:
        out.wait()


def publish(arrays):
    n = len(arrays)
    hbm = pl.BlockSpec(memory_space=pltpu.HBM)
    sem = pltpu.SemaphoreType.DMA((n,))
    return pl.pallas_call(
        publish_kernel,
        out_shape=[jax.ShapeDtypeStruct(a.shape, a.dtype) for a in arrays],
        in_specs=[hbm] * n,
        out_specs=[hbm] * n,
        scratch_shapes=[*(pltpu.VMEM(a.shape, a.dtype) for a in arrays), sem, sem],
        compiler_params=pltpu.CompilerParams(vmem_limit_bytes=VMEM_LIMIT),
    )(*arrays)


def local(tokens, gate_weight, up_weight, down_weight, cotangent):
    ct, fs = tokens.shape
    depth, ff = gate_weight.shape
    fq = ff // 4
    v = pltpu.VMEM
    scratch = [
        v((ct, fs), BF), v((ct, fs), BF),
        v((depth, ff), BF), v((depth, ff), BF), v((ff, depth), BF),
        v((4, 2, fq, depth), BF), v((depth, ff), BF),
        v((4, 2, 4, fs, ct), BF), v((4, 2, 4, fs, ct), BF),
        v((4, 2, 4, 2 * fq, 128), F32), v((4, 4, 2 * fq, 128), F32),
        v((4, 2 * fq, 128), BF), v((4, 2 * fq, 128), BF),
        v((4, 2, 2 * fq, 128), BF), v((4, 2, 2 * fq, 128), BF),
        v((4, 2, 4, fq, 128), F32), v((4, 4, fq, 128), F32),
        v((4, fq, 128), BF), v((4, fq, 128), BF),
        v((4, 2, fq, 128), BF), v((4, 2, fq, 128), BF),
        v((4, fq, 128), F32), v((4, fq, 128), F32),
        v((4, 2, 4, fq, 128), BF), v((4, 2, 2, 4, fq, 128), BF),
        *Scatter.shapes(fs, ct), *Scatter.shapes(fs, ct),
        v((3, ff, depth), BF), v((2, ff, depth), F32), v((2, ct, fs), BF),
        pltpu.SemaphoreType.DMA((10,)),
        pltpu.SemaphoreType.DMA((POOL,)), pltpu.SemaphoreType.DMA((SENDS,)),
    ]
    hbm = pl.BlockSpec(memory_space=pltpu.HBM)
    sds = jax.ShapeDtypeStruct
    results = pl.pallas_call(
        kernel,
        out_shape=[sds((ct, fs), BF), sds((ct, fs), BF), sds((ff, depth), BF),
                   sds((ff, depth), BF), sds((ff, depth), BF)],
        in_specs=[hbm] * 5,
        out_specs=[hbm] * 5,
        scratch_shapes=scratch,
        compiler_params=pltpu.CompilerParams(
            collective_id=0, has_side_effects=True, vmem_limit_bytes=VMEM_LIMIT),
    )(tokens, gate_weight.T.reshape(4, fq, depth), up_weight.T.reshape(4, fq, depth), down_weight, cotangent)
    block_out, input_grad, gate_grad, up_grad, down_grad = publish(results)
    return block_out, input_grad, gate_grad.T, up_grad.T, down_grad


def solution(mesh):
    in_specs = (
        P("tok", ("row", "col")),
        P("row", ("col", "tok")),
        P("row", ("col", "tok")),
        P(("col", "tok"), "row"),
        P("tok", ("row", "col")),
    )
    out_specs = (
        P("tok", ("row", "col")),
        P("tok", ("row", "col")),
        P("row", ("col", "tok")),
        P("row", ("col", "tok")),
        P(("col", "tok"), "row"),
    )
    return jax.shard_map(local, mesh=mesh, in_specs=in_specs, out_specs=out_specs, check_vma=False)
```
